256 devices in a mesh: samp: 16 (over x, y), snp: 16 (over z, core).
Axes of the slice: x: 4, y: 4, z: 8, core: 2. Of those that a mesh axis runs over, the one named last changes fastest.
Arguments:
- genotype: float32 [32768, 8192], P('samp', 'snp'), may hold values from 0 to 2
- effect: float32 [8192, 64], P('snp'), may hold values from -6 to 6
- window_start: int32 [8192], P(('snp', 'samp')), may hold values from 0 to 8191, as said below
- window_end: int32 [8192], P(('snp', 'samp')), may hold values from 1 to 8192, as said below
Outputs:
- band_product: float32 [8192, 64], P(('snp', 'samp'))
The draws below stay inside these ranges and needn't reach their ends.
Inputs may be any that keep to these rules, and one draw needn't show every extreme that they name: window_start[i] <= i and i - window_start[i] <= 511. i < window_end[i] and window_end[i] - i <= 512; some SNP has a window of exactly 1023 SNPs.
All inputs are finite; a program needn't handle non-finite values.
Results may differ from the reference program's by a relative error of at most 0.0003.
Values sent between devices are 32-bit elements; how exact they have to be, the bound alone decides.
No kernel may reach another device: no remote copies, remote signals or barrier semaphores. Data moves between devices by JAX's collectives and lax.ppermute only.
A program may use at most 64 MiB of HBM per device.

```python
import jax
import jax.numpy as jnp
from jax import lax

C = 512
K = 64
M = 8192
NSAMP = 32768


def window_parts(key):
    base = jax.random.fold_in(key, 77)
    positions = jnp.arange(M, dtype=jnp.int32)
    left_reach = jax.random.randint(jax.random.fold_in(base, 1), (M,), 0, C, dtype=jnp.int32)
    right_reach = jax.random.randint(jax.random.fold_in(base, 2), (M,), 0, C, dtype=jnp.int32)
    widest = jax.random.randint(jax.random.fold_in(base, 3), (), C - 1, M - C + 1, dtype=jnp.int32)
    left_reach = jnp.where(positions == widest, C - 1, left_reach)
    right_reach = jnp.where(positions == widest, C - 1, right_reach)
    left_reach = jnp.where(positions == M - 1, 0, left_reach)
    right_reach = jnp.where(positions == 0, 0, right_reach)
    starts = jnp.maximum(positions - left_reach, 0)
    ends = jnp.minimum(positions + 1 + right_reach, M)
    return (starts.astype(jnp.int32), ends.astype(jnp.int32))


def draw_window_start(key, part):
    return window_parts(key)[0]


def draw_window_end(key, part):
    return window_parts(key)[1]


def block_scale(own_key, dims, pieces, low, high):
    level = 1.0
    for axis_at, blocks in pieces:
        draws = jax.random.uniform(jax.random.fold_in(jax.random.fold_in(own_key, 6), axis_at), (blocks,), jnp.float32, low / len(pieces), high / len(pieces))
        level = level * jnp.repeat(jnp.exp(draws), dims[axis_at] // blocks).reshape((-1,) + (1,) * (len(dims) - 1 - axis_at))
    return level


def centred(rng, dims, spread, reach, shards=(), held_as=jnp.bfloat16):
    array = jax.random.normal(rng, dims, jnp.float32) * spread
    if len(shards) > 0:
        array = block_scale(rng, dims, shards, -0.22, 0.18) * array
    return jnp.clip(array, min=-reach, max=reach).astype(held_as)


def setup_inputs(seed: int = 0) -> dict:
    key_list = jax.random.split(jax.random.key(seed), 5)
    return {
        "genotype": jnp.clip(2.0 * jax.random.uniform(key_list[0], (NSAMP, M), jnp.float32) ** block_scale(key_list[0], (NSAMP, M), ((0, 16), (1, 16)), -0.2, 0.2), 0.0, 2.0),
        "effect": centred(key_list[1], (M, K), 1.0, 6.0, ((0, 16),), jnp.float32),
        "window_start": draw_window_start(jax.random.fold_in(key_list[4], 71), 0),
        "window_end": draw_window_end(jax.random.fold_in(key_list[4], 71), 0),
    }


EPSILON = 1e-05

def reference(genotype, effect, window_start, window_end):
    sample_total = genotype.shape[0]
    column_mean = lax.optimization_barrier(jnp.sum(genotype, axis=0)) / sample_total
    column_spread = lax.optimization_barrier(jnp.sum((genotype - column_mean[None, :]) ** 2, axis=0))
    column_scale = lax.rsqrt(column_spread / sample_total + EPSILON)
    padded_geno = jnp.pad(genotype, ((0, 0), (C, C)))
    padded_mean = jnp.pad(column_mean, (C, C))
    padded_scale = jnp.pad(column_scale, (C, C))
    padded_effect = jnp.pad(effect, ((C, C), (0, 0)))

    def one_block(block):
        offset = block * C
        own_cols = lax.dynamic_slice_in_dim(genotype, offset, C, 1)
        wide_cols = lax.dynamic_slice_in_dim(padded_geno, offset, 3 * C, 1)
        cross_products = lax.dot_general(own_cols, wide_cols, (((0,), (0,)), ((), ())), precision=lax.Precision.HIGHEST, preferred_element_type=jnp.float32)
        row_mean = lax.dynamic_slice_in_dim(column_mean, offset, C, 0)
        row_scale = lax.dynamic_slice_in_dim(column_scale, offset, C, 0)
        wide_mean = lax.dynamic_slice_in_dim(padded_mean, offset, 3 * C, 0)
        wide_scale = lax.dynamic_slice_in_dim(padded_scale, offset, 3 * C, 0)
        wide_effect = lax.dynamic_slice_in_dim(padded_effect, offset, 3 * C, 0)
        correlation = (cross_products / sample_total - row_mean[:, None] * wide_mean[None, :]) * (row_scale[:, None] * wide_scale[None, :])
        row_index = offset + jnp.arange(C, dtype=jnp.int32)
        col_index = offset - C + jnp.arange(3 * C, dtype=jnp.int32)
        starts = lax.dynamic_slice_in_dim(window_start, offset, C, 0)
        ends = lax.dynamic_slice_in_dim(window_end, offset, C, 0)
        in_window = (col_index[None, :] >= starts[:, None]) & (col_index[None, :] < ends[:, None])
        band_values = jnp.where(in_window, correlation, jnp.float32(0.0))
        return jnp.dot(band_values, wide_effect, precision=lax.Precision.HIGHEST, preferred_element_type=jnp.float32)
    blocks = lax.map(one_block, jnp.arange(M // C, dtype=jnp.int32))
    return blocks.reshape(M, K)
```

```python
import jax
import jax.numpy as jnp
from jax import lax
from jax.sharding import PartitionSpec as P

EPSILON = 1e-05
HIGH = lax.Precision.HIGH
HIGHEST = lax.Precision.HIGHEST


def gram(left, right):
    return lax.dot_general(
        left, right, (((0,), (0,)), ((), ())), precision=HIGH, preferred_element_type=jnp.float32
    )


def full_dot(left, right, left_dim, right_dim):
    return lax.dot_general(
        left,
        right,
        (((left_dim,), (right_dim,)), ((), ())),
        precision=HIGHEST,
        preferred_element_type=jnp.float32,
    )


def body(genotype, effect, window_start, window_end):
    samp_count = lax.axis_size("samp")
    snp_count = lax.axis_size("snp")
    samples_here, width = genotype.shape
    columns = effect.shape[1]
    row_count = width // samp_count
    sample_total = samples_here * samp_count
    half = samples_here // 2
    block = lax.axis_index("snp")
    odd = lax.rem(block, 2)
    chip_pairs = [(i, i ^ 1) for i in range(snp_count)]
    cross_pairs = [(i, i + 1) for i in range(1, snp_count - 1, 2)]
    cross_pairs += [(i + 1, i) for i in range(1, snp_count - 1, 2)]

    sent = lax.dynamic_slice_in_dim(genotype, odd * half, half, 0)
    kept = lax.dynamic_slice_in_dim(genotype, (1 - odd) * half, half, 0)
    across = lax.ppermute(sent, "snp", cross_pairs)
    mate = lax.ppermute(genotype, "snp", chip_pairs)

    shard_mean = jnp.sum(genotype, axis=0) / samples_here
    shard_spread = jnp.sum((genotype - shard_mean[None, :]) ** 2, axis=0)
    pack = jnp.concatenate(
        [
            shard_mean,
            shard_spread,
            window_start.astype(jnp.float32),
            window_end.astype(jnp.float32),
            jnp.zeros((2 * row_count,), jnp.float32),
        ]
    ).reshape(1, -1, 128)
    packs = lax.all_to_all(
        jnp.broadcast_to(pack, (samp_count,) + pack.shape[1:]), "samp", 0, 0
    ).reshape(samp_count, -1)
    means = packs[:, :width]
    spreads = packs[:, width : 2 * width]
    starts = packs[:, 2 * width : 2 * width + row_count].reshape(width)
    ends = packs[:, 2 * width + row_count : 2 * width + 2 * row_count].reshape(width)
    mean = jnp.sum(means, axis=0) / samp_count
    spread = jnp.sum(spreads, axis=0) + samples_here * jnp.sum((means - mean[None, :]) ** 2, axis=0)
    scale = lax.rsqrt(spread / sample_total + EPSILON)
    scaled = effect.T * scale[None, :]
    own_info = jnp.concatenate(
        [scaled, mean[None, :], starts[None, :], ends[None, :], jnp.zeros((5, width), jnp.float32)]
    )
    mate_info = lax.ppermute(own_info, "snp", chip_pairs)
    cross_info = lax.ppermute(own_info, "snp", cross_pairs)

    def column_index(which):
        return (which * width + jnp.arange(width, dtype=jnp.int32)).astype(jnp.float32)

    def masked(products, row_starts, row_ends, column_block):
        index = column_index(column_block)
        inside = (index[None, :] >= row_starts[:, None]) & (index[None, :] < row_ends[:, None])
        return jnp.where(inside, products, jnp.float32(0.0))

    shift = shard_mean - mean
    own_products = gram(genotype - shard_mean[None, :], genotype - shard_mean[None, :])
    own_products = own_products + samples_here * shift[:, None] * shift[None, :]
    mate_products = gram(genotype - mean[None, :], mate - mate_info[columns][None, :])
    cross_products = gram(kept - mean[None, :], across - cross_info[columns][None, :])
    cross_block = block + 2 * odd - 1
    own_sum = (
        full_dot(masked(own_products, starts, ends, block), scaled, 1, 1)
        + full_dot(
            masked(mate_products, starts, ends, block + 1 - 2 * odd), mate_info[:columns], 1, 1
        )
        + full_dot(masked(cross_products, starts, ends, cross_block), cross_info[:columns], 1, 1)
    )
    cross_starts = cross_info[columns + 1]
    cross_ends = cross_info[columns + 2]
    index = column_index(block)
    inside = (index[:, None] >= cross_starts[None, :]) & (index[:, None] < cross_ends[None, :])
    cross_sum = full_dot(jnp.where(inside, cross_products, jnp.float32(0.0)), scaled, 0, 1)
    both = jnp.concatenate([own_sum, cross_sum], axis=1).reshape(samp_count, row_count, 2 * columns)
    parts = jnp.sum(lax.all_to_all(both, "samp", 0, 0), axis=0)
    from_across = lax.ppermute(parts[:, columns:], "snp", cross_pairs)
    row_first = lax.axis_index("samp") * row_count
    row_scale = lax.dynamic_slice_in_dim(scale, row_first, row_count, 0) / sample_total
    return (parts[:, :columns] + from_across) * row_scale[:, None]


def solution(mesh):
    placed = (P("samp", "snp"), P("snp", None), P(("snp", "samp")), P(("snp", "samp")))
    return jax.shard_map(
        body, mesh=mesh, in_specs=placed, out_specs=P(("snp", "samp"), None), check_vma=False
    )
```

```python
import functools

import jax
import jax.numpy as jnp
from jax import lax
from jax.experimental import pallas as pl
from jax.experimental.pallas import tpu as pltpu
from jax.sharding import PartitionSpec as P

EPSILON = 1e-05
F32 = jnp.float32
LANES = 128
LAST_ROWS = 256
STEP_ROWS = 1024
VMEM = pl.BlockSpec(memory_space=pltpu.VMEM)
SMEM = pl.BlockSpec(memory_space=pltpu.SMEM)
ANY = pl.BlockSpec(memory_space=pl.ANY)


def split(values):
    high = values.astype(jnp.bfloat16)
    return high, (values - high.astype(F32)).astype(jnp.bfloat16)


def dot(left, right, left_dim, right_dim):
    return lax.dot_general(
        left, right, (((left_dim,), (right_dim,)), ((), ())), preferred_element_type=F32
    )


def three_dots(left, right, left_dim, right_dim):
    (left_high, left_low), (right_high, right_low) = left, right
    return (
        dot(left_high, right_high, left_dim, right_dim)
        + dot(left_high, right_low, left_dim, right_dim)
        + dot(left_low, right_high, left_dim, right_dim)
    )


def column_means(ref, start, rows):
    return jnp.sum(ref[pl.ds(start, rows), :], axis=0, keepdims=True) / rows


def stat_kernel(place, geno, starts, ends, sent, pack, means):
    del sent
    rows, width = geno.shape
    values = geno[...]
    mean = jnp.sum(values, axis=0, keepdims=True) / rows
    spread = jnp.sum((values - mean) ** 2, axis=0, keepdims=True)
    means[...] = jnp.broadcast_to(mean, means.shape)
    tiles = width // LANES
    here = starts.shape[1]
    slot = (
        lax.broadcasted_iota(jnp.int32, (tiles, LANES), 0) * (LANES // here)
        + lax.broadcasted_iota(jnp.int32, (tiles, LANES), 1) // here
    )
    mine = slot == place[0]

    def spread_out(ref):
        row = jnp.concatenate([ref[...].astype(F32)] * (LANES // here), axis=1)
        return jnp.where(mine, jnp.broadcast_to(row, (tiles, LANES)), jnp.float32(0.0))

    rows_out = [vector[:, t * LANES : (t + 1) * LANES] for vector in (mean, spread) for t in range(tiles)]
    rows_out += [spread_out(starts), spread_out(ends)]
    pack[...] = jnp.broadcast_to(jnp.concatenate(rows_out, axis=0)[None], pack.shape)


def combine_kernel(place, packs, geno, effect, own_products, later, own, *, samples_here):
    del own_products
    count, _, _ = packs.shape
    width = geno.shape[1]
    columns = effect.shape[0]
    tiles = width // LANES
    total = samples_here * count
    values = packs[...]
    means = values[:, :tiles]
    mean = jnp.sum(means, axis=0) / count
    spread = jnp.sum(values[:, tiles : 2 * tiles], axis=0)
    spread = spread + samples_here * jnp.sum((means - mean[None]) ** 2, axis=0)
    scale = lax.rsqrt(spread / total + EPSILON)
    starts = jnp.sum(values[:, 2 * tiles : 3 * tiles], axis=0)
    ends = jnp.sum(values[:, 3 * tiles :], axis=0)

    def as_row(tiled):
        return jnp.concatenate([tiled[t : t + 1] for t in range(tiles)], axis=1)

    info = jnp.concatenate(
        [as_row(mean), as_row(scale), as_row(starts), as_row(ends), jnp.zeros((4, width), F32)], axis=0
    )
    own[:columns] = effect[...]
    own[columns:] = info
    rows = later.shape[0] - own.shape[0]
    begin = pl.multiple_of(place[3], 8)
    later[:rows] = geno[pl.ds(begin, rows), :]
    later[rows : rows + columns] = effect[...]
    later[rows + columns :] = info


def own_kernel(geno, means, products, cross):
    rows = geno.shape[0]
    mean = means[:1]
    products[...] = jnp.zeros_like(products)
    cross[...] = jnp.zeros_like(cross)

    def step(i, carry):
        high, low = split(geno[pl.ds(pl.multiple_of(i * STEP_ROWS, STEP_ROWS), STEP_ROWS), :] - mean)
        products[...] += dot(high, high, 0, 0)
        cross[...] += dot(high, low, 0, 0)
        return carry

    lax.fori_loop(0, rows // STEP_ROWS, step, 0)
    products[...] += cross[...] + cross[...].T


def accumulate(products, left, right, reaches_right):
    half = products.shape[0] // 2
    low, high = slice(0, half), slice(half, 2 * half)
    every = slice(0, 2 * half)

    def add(rows, cols):
        part = three_dots(
            [piece[:, rows] for piece in left], [piece[:, cols] for piece in right], 0, 0
        )
        products[rows, cols] += part

    @pl.when(reaches_right)
    def _():
        add(every, low)
        add(high, high)

    @pl.when(jnp.logical_not(reaches_right))
    def _():
        add(low, every)
        add(high, high)


def pair_kernel(place, geno, other, products, means, *, start_at, right_parity):
    rows = other.shape[0]
    step_rows = min(rows, STEP_ROWS)
    begin = 0 if start_at is None else pl.multiple_of(place[start_at], 8)
    own_mean = column_means(geno, begin, rows)
    other_mean = column_means(other, 0, rows)
    means[...] = jnp.concatenate(
        [own_mean, other_mean, jnp.zeros((6, means.shape[1]), F32)], axis=0
    )
    products[...] = jnp.zeros_like(products)

    def step(i, carry):
        offset = pl.multiple_of(i * step_rows, step_rows)
        left = split(geno[pl.ds(begin + offset, step_rows), :] - own_mean)
        right = split(other[pl.ds(offset, step_rows), :] - other_mean)
        accumulate(products, left, right, place[1] == right_parity)
        return carry

    lax.fori_loop(0, rows // step_rows, step, 0)


def inside(first, shape, dim, starts, ends):
    index = (first + lax.broadcasted_iota(jnp.int32, shape, dim)).astype(F32)
    return (index >= starts) & (index < ends)


def near_kernel(
    place, own_products, means, mate_products, mate_means, own, mate, out, *, columns, samples_here, total
):
    width = own_products.shape[0]
    block, odd = place[2], place[1]
    info = own[columns : columns + 4]
    mean, scale = info[0:1], info[1:2]
    mate_mean, mate_scale = mate[columns : columns + 1], mate[columns + 1 : columns + 2]
    shift = means[0:1] - mean
    mate_side = mate_means[0:1] - mean
    across = jnp.concatenate([info, shift, mate_side, jnp.zeros((2, width), F32)], axis=0).T
    row_scale = across[:, 1:2] * (1.0 / total)
    starts, ends = across[:, 2:3], across[:, 3:4]

    def part(products, row_shift, col_shift, col_scale, block_at, source):
        centred = products[...] + (samples_here * row_shift) * col_shift
        keep = inside(block_at * width, (width, width), 1, starts, ends)
        band = jnp.where(keep, centred * (row_scale * col_scale), jnp.float32(0.0))
        return three_dots(split(band), split(source[:columns]), 1, 1)

    out[...] = part(own_products, across[:, 4:5], shift, scale, block, own) + part(
        mate_products,
        across[:, 5:6],
        mate_means[1:2] - mate_mean,
        mate_scale,
        block + 1 - 2 * odd,
        mate,
    )


def far_kernel(
    place, geno, products_in, means, later, own, near, out, products, *, columns, first_rows, total
):
    width = own.shape[1]
    block, odd = place[2], place[1]
    rows = later.shape[0] - own.shape[0]
    begin = pl.multiple_of(place[5], 8)
    mean = own[columns : columns + 1]
    info = later[rows + columns : rows + columns + 4]
    far_mean, far_scale = info[0:1], info[1:2]
    products[...] = products_in[...]
    left = split(geno[pl.ds(begin, rows), :] - mean)
    right = split(later[:rows] - far_mean)
    accumulate(products, left, right, odd == 1)
    row_shift = means[0:1] - mean
    col_shift = means[1:2] - far_mean
    across = jnp.concatenate(
        [own[columns : columns + 4], row_shift, jnp.zeros((3, width), F32)], axis=0
    ).T
    centred = products[...] + (first_rows * across[:, 4:5]) * col_shift
    correlation = centred * ((across[:, 1:2] * (1.0 / total)) * far_scale)
    shape = (width, width)
    far_block = block + 2 * odd - 1
    keep_own = inside(far_block * width, shape, 1, across[:, 2:3], across[:, 3:4])
    keep_far = inside(block * width, shape, 0, info[2:3], info[3:4])
    own_band = jnp.where(keep_own, correlation, jnp.float32(0.0))
    far_band = jnp.where(keep_far, correlation, jnp.float32(0.0))
    own_sum = near[...] + three_dots(
        split(own_band), split(later[rows : rows + columns]), 1, 1
    )
    far_sum = three_dots(split(own[:columns]), split(far_band), 1, 0).T
    count, _, piece_rows, lanes = out.shape

    def pieces(values):
        parts = values.reshape(count, 2, piece_rows, columns)
        return jnp.concatenate([parts[:, 0], parts[:, 1]], axis=-1)

    out[:, 1 - odd] = pieces(own_sum)
    out[:, odd] = pieces(far_sum)


def last_kernel(parts, out):
    total = jnp.sum(parts[...], axis=0)
    rows, columns = out.shape
    out[: rows // 2] = total[:, :columns]
    out[rows // 2 :] = total[:, columns:]


def call(kernel, shapes, specs, scratch=(), flops=1000, **sizes):
    outs = [jax.ShapeDtypeStruct(shape, F32) for shape in shapes]
    return pl.pallas_call(
        functools.partial(kernel, **sizes),
        out_shape=outs,
        in_specs=specs,
        out_specs=[VMEM] * len(outs),
        scratch_shapes=list(scratch),
        compiler_params=pltpu.CompilerParams(vmem_limit_bytes=40 * 1024 * 1024),
        cost_estimate=pl.CostEstimate(flops=flops, bytes_accessed=1000, transcendentals=0),
        name=kernel.__name__,
    )


def body(genotype, effect, window_start, window_end):
    samp_count = lax.axis_size("samp")
    snp_count = lax.axis_size("snp")
    samples_here, width = genotype.shape
    columns = effect.shape[1]
    row_count = width // samp_count
    total = samples_here * samp_count
    half = samples_here // 2
    first_rows = half - LAST_ROWS
    info_rows = columns + 8
    gram_flops = 6 * width * width * samples_here
    samp = lax.axis_index("samp")
    block = lax.axis_index("snp")
    odd = lax.rem(block, 2)
    sent_at = odd * half
    kept_at = (1 - odd) * half
    place = jnp.stack(
        [samp, odd, block, sent_at + first_rows, kept_at, kept_at + first_rows]
    ).astype(jnp.int32)
    chip_pairs = [(i, i ^ 1) for i in range(snp_count)]
    cross = [(i, (i + 1) % snp_count) for i in range(1, snp_count, 2)]
    cross_pairs = [pair for i, j in cross[:-1] for pair in ((i, j), (j, i))]
    effect_rows = effect.T

    sent = lax.dynamic_slice_in_dim(genotype, sent_at, first_rows, 0)
    first = lax.ppermute(sent, "snp", cross_pairs)
    mate = lax.ppermute(genotype, "snp", chip_pairs)
    pack, means = call(
        stat_kernel,
        [(samp_count, 4 * width // LANES, LANES), (8, width)],
        [SMEM, VMEM, VMEM, VMEM, ANY],
    )(place, genotype, window_start[None], window_end[None], sent)
    packs = lax.all_to_all(pack, "samp", 0, 0)
    own_products = call(
        own_kernel, [(width, width)], [VMEM] * 2, [pltpu.VMEM((width, width), F32)], flops=gram_flops
    )(genotype, means)[0]
    mate_products, mate_means = call(
        pair_kernel,
        [(width, width), (8, width)],
        [SMEM] + [VMEM] * 2,
        start_at=None,
        right_parity=0,
        flops=gram_flops,
    )(place, genotype, mate)
    later, own = call(
        combine_kernel,
        [(LAST_ROWS + info_rows, width), (info_rows, width)],
        [SMEM] + [VMEM] * 3 + [ANY],
        samples_here=samples_here,
    )(place, packs, genotype, effect_rows, own_products)
    later = lax.ppermute(later, "snp", cross_pairs)
    mate_info = lax.ppermute(own, "snp", chip_pairs)
    near = call(
        near_kernel,
        [(width, columns)],
        [SMEM] + [VMEM] * 6,
        columns=columns,
        samples_here=samples_here,
        total=total,
    )(place, own_products, means, mate_products, mate_means, own, mate_info)[0]
    first_products, first_means = call(
        pair_kernel,
        [(width, width), (8, width)],
        [SMEM] + [VMEM] * 2,
        start_at=4,
        right_parity=1,
    )(place, genotype, first)
    sums = call(
        far_kernel,
        [(samp_count, 2, row_count // 2, 2 * columns)],
        [SMEM] + [VMEM] * 6,
        [pltpu.VMEM((width, width), F32)],
        columns=columns,
        first_rows=first_rows,
        total=total,
    )(place, genotype, first_products, first_means, later, own, near)[0]
    groups = [[s * snp_count + i for s in range(samp_count) for i in pair] for pair in cross]
    parts = lax.all_to_all(
        sums.reshape(2 * samp_count, row_count // 2, 2 * columns),
        ("samp", "snp"),
        0,
        0,
        axis_index_groups=groups,
    )
    return call(last_kernel, [(row_count, columns)], [VMEM])(parts)[0]


def solution(mesh):
    placed = (P("samp", "snp"), P("snp", None), P(("snp", "samp")), P(("snp", "samp")))
    return jax.shard_map(
        body, mesh=mesh, in_specs=placed, out_specs=P(("snp", "samp"), None), check_vma=False
    )
```

```python
import functools

import jax
import jax.numpy as jnp
from jax import lax
from jax.experimental import pallas as pl
from jax.experimental.pallas import tpu as pltpu
from jax.sharding import PartitionSpec as P

EPSILON = 1e-05
F32 = jnp.float32
BF16 = jnp.bfloat16
LANES = 128
READS = 4
VMEM = pl.BlockSpec(memory_space=pltpu.VMEM)
HBM = pl.BlockSpec(memory_space=pltpu.HBM)
ANY = pl.BlockSpec(memory_space=pl.ANY)


def split(values):
    high = values.astype(BF16)
    return high, (values - high.astype(F32)).astype(BF16)


def dot(left, right, left_dim, right_dim):
    return lax.dot_general(
        left, right, (((left_dim,), (right_dim,)), ((), ())), preferred_element_type=F32
    )


def three_dots(left, right, left_dim, right_dim):
    (left_high, left_low), (right_high, right_low) = left, right
    return (
        dot(left_high, right_high, left_dim, right_dim)
        + dot(left_high, right_low, left_dim, right_dim)
        + dot(left_low, right_high, left_dim, right_dim)
    )


def position(geno_rows):
    block = lax.axis_index("snp")
    odd = lax.rem(block, 2)
    half = geno_rows // 2
    return block, odd, odd * half, (1 - odd) * half


def column_sum(values):
    return jnp.sum(values, axis=0, keepdims=True)


def copies_in(source, begin, target, sems, pieces):
    rows = target.shape[0] // pieces
    return [
        pltpu.make_async_copy(
            source.at[pl.ds(pl.multiple_of(begin + i * rows, 8), rows)],
            target.at[pl.ds(i * rows, rows)],
            sems.at[i],
        )
        for i in range(pieces)
    ]


def start(*groups):
    for group in groups:
        for copy in group:
            copy.start()


def finish(*copies):
    for copy in copies:
        copy.wait()


def copy_kernel(geno, out, sems):
    sent_at = position(geno.shape[0])[2]
    copies = copies_in(geno, sent_at, out, sems, READS)
    start(copies)
    finish(*copies)


def stat_kernel(
    geno,
    starts,
    ends,
    sent,
    pack,
    means,
    products,
    values,
    edges,
    sems,
    edge_sems,
):
    del sent
    rows, width = values.shape
    piece = rows // READS
    copies = copies_in(geno, 0, values, sems, READS)
    edge_copies = [
        pltpu.make_async_copy(ref, edges.at[pl.ds(i, 1)], edge_sems.at[i])
        for i, ref in enumerate((starts, ends))
    ]
    start(copies, edge_copies)
    for i, copy in enumerate(copies):
        copy.wait()
        at = slice(i * piece, (i + 1) * piece)
        if i == 0:
            centre = column_sum(values[at]) / piece
        near_centre = values[at] - centre
        part, squares = column_sum(near_centre), column_sum(near_centre * near_centre)
        high, low = split(near_centre)
        product = dot(high, high * 0.5, 0, 0) + dot(high, low, 0, 0)
        if i == 0:
            total, spread = part, squares
            products[...] = product
        else:
            total, spread = total + part, spread + squares
            products[...] += product
    offset = total / rows
    mean = centre + offset
    spread = spread - rows * offset * offset
    offsets = jnp.broadcast_to(offset, (8, width))
    products[...] += products[...].T - (rows * offsets.T[:, 0:1]) * offset
    means[...] = jnp.broadcast_to(mean, means.shape)
    tiles = width // LANES
    here = edges.shape[1]
    slot = (
        lax.broadcasted_iota(jnp.int32, (tiles, LANES), 0) * (LANES // here)
        + lax.broadcasted_iota(jnp.int32, (tiles, LANES), 1) // here
    )
    mine = slot == lax.axis_index("samp")
    finish(*edge_copies)

    def spread_out(i):
        row = jnp.concatenate([edges[i : i + 1].astype(F32)] * (LANES // here), axis=1)
        return jnp.where(mine, jnp.broadcast_to(row, (tiles, LANES)), jnp.float32(0.0))

    rows_out = [
        vector[:, t * LANES : (t + 1) * LANES] for vector in (mean, spread) for t in range(tiles)
    ]
    rows_out += [spread_out(0), spread_out(1)]
    pack[...] = jnp.broadcast_to(jnp.concatenate(rows_out, axis=0)[None], pack.shape)


def combine_kernel(packs, effect, mate_means, own, *, samples_here):
    del mate_means
    count, _, _ = packs.shape
    columns, width = effect.shape
    tiles = width // LANES
    total = samples_here * count
    values = packs[...]
    means = values[:, :tiles]
    mean = jnp.sum(means, axis=0) / count
    spread = jnp.sum(values[:, tiles : 2 * tiles], axis=0)
    spread = spread + samples_here * jnp.sum((means - mean[None]) ** 2, axis=0)
    scale = lax.rsqrt(spread / total + EPSILON)
    starts = jnp.sum(values[:, 2 * tiles : 3 * tiles], axis=0)
    ends = jnp.sum(values[:, 3 * tiles :], axis=0)

    def as_row(tiled):
        return jnp.concatenate([tiled[t : t + 1] for t in range(tiles)], axis=1)

    info = jnp.concatenate(
        [as_row(mean), as_row(scale), as_row(starts), as_row(ends), jnp.zeros((4, width), F32)],
        axis=0,
    )
    own[:columns] = effect[...]
    own[columns:] = info


def in_triangle(width, reaches_right, work):
    lower, upper, every = slice(0, width // 2), slice(width // 2, width), slice(0, width)

    @pl.when(reaches_right)
    def _():
        work([(lower, lower), (upper, every)])

    @pl.when(jnp.logical_not(reaches_right))
    def _():
        work([(lower, every), (upper, upper)])


def block_dots(left, right, rows, cols):
    return three_dots([part[:, rows] for part in left], [part[:, cols] for part in right], 0, 0)


def mate_kernel(
    geno, mate, means, out, mate_means, values, mate_values, products, sems, mate_sems, out_sem
):
    rows, width = values.shape
    odd = position(rows)[1]
    half = width // 2
    writes = [
        pltpu.make_async_copy(
            products.at[pl.ds(i * half, half)], out.at[pl.ds(i * half, half)], out_sem.at[i]
        )
        for i in range(2)
    ]
    products[:half, half:] = jnp.zeros((half, half), F32)
    products[half:, :half] = jnp.zeros((half, half), F32)
    copies = copies_in(geno, 0, values, sems, READS)
    mate_copies = copies_in(mate, 0, mate_values, mate_sems, READS)
    for copy, mate_copy in zip(copies, mate_copies):
        copy.start()
        mate_copy.start()
    mean = means[0:1]
    piece = rows // READS
    centre = None
    total = None
    for i in range(READS):
        at = slice(i * piece, (i + 1) * piece)
        copies[i].wait()
        mate_copies[i].wait()
        part = column_sum(mate_values[at])
        total = part if total is None else total + part
        centre = part / piece if centre is None else centre

        def work(blocks):
            left, right = split(values[at] - mean), split(mate_values[at] - centre)
            for block_rows, block_cols in blocks:
                product = block_dots(left, right, block_rows, block_cols)
                if i == 0:
                    products[block_rows, block_cols] = product
                else:
                    products[block_rows, block_cols] += product
                if i == READS - 1:
                    writes[block_rows.start // half].start()

        in_triangle(width, odd == 0, work)
    mate_means[...] = jnp.broadcast_to(total / rows, mate_means.shape)
    finish(*writes)


def inside(first, shape, dim, starts, ends):
    index = (first + lax.broadcasted_iota(jnp.int32, shape, dim)).astype(F32)
    return (index >= starts) & (index < ends)


def near_kernel(
    geno,
    own_products,
    means,
    mate_products,
    mate_means,
    own,
    mate,
    out,
    kept,
    near_products,
    mate_sem,
    kept_sems,
    *,
    columns,
    samples_here,
    total,
):
    width = own_products.shape[0]
    block, odd, _, kept_at = position(samples_here)
    mate_copies = copies_in(mate_products, 0, near_products, mate_sem, 1)
    kept_copies = copies_in(geno, kept_at, kept, kept_sems, 2)
    start(mate_copies, kept_copies)
    info = own[columns : columns + 4]
    mean, scale = info[0:1], info[1:2]
    mate_mean, mate_scale = mate[columns : columns + 1], mate[columns + 1 : columns + 2]
    shift = means[0:1] - mean
    across = jnp.concatenate([info, shift, jnp.zeros((3, width), F32)], axis=0).T
    row_shift = samples_here * across[:, 4:5]
    row_scale = across[:, 1:2] * (1.0 / total)
    starts, ends = across[:, 2:3], across[:, 3:4]

    def part(at, cols, ref, col_shift, col_scale, block_at, source):
        centred = ref[at, cols] + row_shift[at] * col_shift[:, cols]
        first_column = block_at * width + cols.start
        keep = inside(first_column, centred.shape, 1, starts[at], ends[at])
        band = jnp.where(keep, centred * (row_scale[at] * col_scale[:, cols]), jnp.float32(0.0))
        return three_dots(split(band), split(source[:columns, cols]), 1, 1)

    every = slice(0, width)
    out[...] = part(every, every, own_products, shift, scale, block, own)
    mate_shift = mate_means[0:1] - mate_mean

    finish(*mate_copies)

    def mate_work(blocks):
        for at, cols in blocks:
            out[at] += part(
                at, cols, near_products, mate_shift, mate_scale, block + 1 - 2 * odd, mate
            )

    in_triangle(width, odd == 0, mate_work)
    finish(*kept_copies)


def cross_kernel(kept, means, across, products, cross_means, others, other_sems):
    rows, width = others.shape
    odd = position(rows)[1]
    pieces = other_sems.shape[0]
    piece = rows // pieces
    other_copies = copies_in(across, 0, others, other_sems, pieces)
    start(other_copies)
    mean = means[0:1]
    centre = None
    for i in range(pieces):
        at = slice(i * piece, (i + 1) * piece)
        other_copies[i].wait()
        part = column_sum(others[at])
        if i == 0:
            centre = part / piece
            other_sum = part
        else:
            other_sum = other_sum + part

        def work(blocks):
            left = kept[at] - mean
            total = column_sum(left)
            if i == 0:
                cross_means[0:1] = total
            else:
                cross_means[0:1] += total
            left, right = split(left), split(others[at] - centre)
            for block_rows, block_cols in blocks:
                product = block_dots(left, right, block_rows, block_cols)
                if i == 0:
                    products[block_rows, block_cols] = product
                else:
                    products[block_rows, block_cols] += product

        in_triangle(width, odd == 1, work)
    cross_means[1:2] = other_sum / rows
    cross_means[2:3] = centre
    cross_means[3:] = jnp.zeros((5, width), F32)


def far_kernel(
    products,
    means,
    cross_means,
    far,
    own,
    near,
    out,
    own_sum,
    far_sum,
    *,
    columns,
    total,
    samples_here,
):
    width = own.shape[1]
    rows = samples_here // 2
    block, odd = position(samples_here)[:2]
    info = far[columns : columns + 4]
    far_mean, far_scale = info[0:1], info[1:2]
    shift = means[0:1] - own[columns : columns + 1]
    across = jnp.concatenate(
        [own[columns : columns + 4], cross_means[0:1], shift, jnp.zeros((2, width), F32)], axis=0
    ).T
    row_scale = across[:, 1:2] * (1.0 / total)
    left_sum, row_shift = across[:, 4:5], rows * across[:, 5:6]
    centre_shift = cross_means[2:3] - far_mean
    other_shift = cross_means[1:2] - far_mean
    far_block = block + 2 * odd - 1
    count, _, piece_rows, lanes = out.shape

    def pieces(values):
        parts = values.reshape(count, 2, piece_rows, columns)
        return jnp.concatenate([parts[:, 0], parts[:, 1]], axis=-1)

    far_sum[...] = jnp.zeros_like(far_sum)

    def work(blocks):
        for at, cols in blocks:
            centred = products[at, cols] + left_sum[at] * centre_shift[:, cols]
            centred = centred + row_shift[at] * other_shift[:, cols]
            correlation = centred * (row_scale[at] * far_scale[:, cols])
            keep_own = inside(
                far_block * width + cols.start, centred.shape, 1, across[at, 2:3], across[at, 3:4]
            )
            keep_far = inside(
                block * width + at.start, centred.shape, 0, info[2:3, cols], info[3:4, cols]
            )
            own_band = jnp.where(keep_own, correlation, jnp.float32(0.0))
            far_band = jnp.where(keep_far, correlation, jnp.float32(0.0))
            own_sum[at] = near[at] + three_dots(
                split(own_band), split(far[:columns, cols]), 1, 1
            )
            far_sum[:, cols] += three_dots(split(own[:columns, at]), split(far_band), 1, 0)

    in_triangle(width, odd == 1, work)
    out[:, 1 - odd] = pieces(own_sum[...])
    out[:, odd] = pieces(far_sum[...].T)


def last_kernel(parts, out):
    total = jnp.sum(parts[...], axis=0)
    rows, columns = out.shape
    out[: rows // 2] = total[:, :columns]
    out[rows // 2 :] = total[:, columns:]


def call(kernel, shapes, specs, scratch=(), flops=1000, out_specs=None, **sizes):
    outs = [shape if hasattr(shape, "dtype") else jax.ShapeDtypeStruct(shape, F32) for shape in shapes]
    return pl.pallas_call(
        functools.partial(kernel, **sizes),
        out_shape=outs,
        in_specs=specs,
        out_specs=out_specs or [VMEM] * len(outs),
        scratch_shapes=list(scratch),
        compiler_params=pltpu.CompilerParams(vmem_limit_bytes=48 * 1024 * 1024),
        cost_estimate=pl.CostEstimate(flops=flops, bytes_accessed=1000, transcendentals=0),
        name=kernel.__name__,
    )


def body(genotype, effect, window_start, window_end):
    samp_count = lax.axis_size("samp")
    snp_count = lax.axis_size("snp")
    samples_here, width = genotype.shape
    columns = effect.shape[1]
    row_count = width // samp_count
    total = samples_here * samp_count
    half = samples_here // 2
    info_rows = columns + 8
    gram_flops = 6 * width * width * samples_here
    chip_pairs = [(i, i ^ 1) for i in range(snp_count)]
    cross = [(i, (i + 1) % snp_count) for i in range(1, snp_count, 2)]
    cross_pairs = [pair for i, j in cross[:-1] for pair in ((i, j), (j, i))]
    effect_rows = effect.T
    square = (width, width)
    whole = (samples_here, width)
    in_hbm = pltpu.with_memory_space_constraint(genotype, pltpu.HBM)
    reads = pltpu.SemaphoreType.DMA((READS,))

    sent = call(copy_kernel, [(half, width)], [HBM], [reads])(in_hbm)[0]
    across = lax.ppermute(sent, "snp", cross_pairs)
    mate = lax.ppermute(genotype, "snp", chip_pairs)
    pack, means, own_products = call(
        stat_kernel,
        [
            (samp_count, 4 * width // LANES, LANES),
            (8, width),
            square,
        ],
        [HBM, HBM, HBM, ANY],
        [
            pltpu.VMEM(whole, F32),
            pltpu.VMEM((2, row_count), jnp.int32),
            reads,
            pltpu.SemaphoreType.DMA((2,)),
        ],
    )(
        in_hbm,
        pltpu.with_memory_space_constraint(window_start[None], pltpu.HBM),
        pltpu.with_memory_space_constraint(window_end[None], pltpu.HBM),
        sent,
    )
    packs = lax.all_to_all(pack, "samp", 0, 0)
    mate_products, mate_means = call(
        mate_kernel,
        [pltpu.HBM(square, F32), (8, width)],
        [HBM, HBM, VMEM],
        [
            pltpu.VMEM(whole, F32),
            pltpu.VMEM(whole, F32),
            pltpu.VMEM(square, F32),
            reads,
            reads,
            pltpu.SemaphoreType.DMA((2,)),
        ],
        out_specs=[HBM, VMEM],
        flops=2 * gram_flops,
    )(in_hbm, pltpu.with_memory_space_constraint(mate, pltpu.HBM), means)
    own = call(
        combine_kernel,
        [(info_rows, width)],
        [VMEM] * 2 + [ANY],
        samples_here=samples_here,
    )(packs, effect_rows, mate_means)[0]
    far = lax.ppermute(own, "snp", cross_pairs)
    mate_info = lax.ppermute(own, "snp", chip_pairs)
    near, kept = call(
        near_kernel,
        [(width, columns), (half, width)],
        [HBM, VMEM, VMEM, HBM] + [VMEM] * 3,
        [pltpu.VMEM(square, F32), pltpu.SemaphoreType.DMA((1,)), pltpu.SemaphoreType.DMA((2,))],
        columns=columns,
        samples_here=samples_here,
        total=total,
    )(
        in_hbm,
        own_products,
        means,
        pltpu.with_memory_space_constraint(mate_products, pltpu.HBM),
        mate_means,
        own,
        mate_info,
    )
    cross_products, cross_means = call(
        cross_kernel,
        [square, (8, width)],
        [VMEM, VMEM, HBM],
        [pltpu.VMEM((half, width), F32), pltpu.SemaphoreType.DMA((2,))],
        flops=gram_flops,
    )(kept, means, pltpu.with_memory_space_constraint(across, pltpu.HBM))
    sums = call(
        far_kernel,
        [(samp_count, 2, row_count // 2, 2 * columns)],
        [VMEM] * 6,
        [pltpu.VMEM((width, columns), F32), pltpu.VMEM((columns, width), F32)],
        columns=columns,
        total=total,
        samples_here=samples_here,
    )(cross_products, means, cross_means, far, own, near)[0]
    groups = [[s * snp_count + i for s in range(samp_count) for i in pair] for pair in cross]
    parts = lax.all_to_all(
        sums.reshape(2 * samp_count, row_count // 2, 2 * columns),
        ("samp", "snp"),
        0,
        0,
        axis_index_groups=groups,
    )
    return call(last_kernel, [(row_count, columns)], [VMEM])(parts)[0]


def solution(mesh):
    placed = (P("samp", "snp"), P("snp", None), P(("snp", "samp")), P(("snp", "samp")))
    return jax.shard_map(
        body, mesh=mesh, in_specs=placed, out_specs=P(("snp", "samp"), None), check_vma=False
    )
```

```python
import functools

import jax
import jax.numpy as jnp
from jax import lax
from jax.experimental import pallas as pl
from jax.experimental.pallas import tpu as pltpu
from jax.sharding import PartitionSpec as P

EPSILON = 1e-05
F32 = jnp.float32
BF16 = jnp.bfloat16
LANES = 128
READS = 4
FAR_READS = 2
LAST_ROWS = 64
VMEM = pl.BlockSpec(memory_space=pltpu.VMEM)
HBM = pl.BlockSpec(memory_space=pltpu.HBM)
ANY = pl.BlockSpec(memory_space=pl.ANY)


def split(values):
    high = values.astype(BF16)
    return high, (values - high.astype(F32)).astype(BF16)


def dot(left, right, left_dim, right_dim):
    return lax.dot_general(
        left, right, (((left_dim,), (right_dim,)), ((), ())), preferred_element_type=F32
    )


def three_dots(left, right, left_dim, right_dim):
    (left_high, left_low), (right_high, right_low) = left, right
    return (
        dot(left_high, right_high, left_dim, right_dim)
        + dot(left_high, right_low, left_dim, right_dim)
        + dot(left_low, right_high, left_dim, right_dim)
    )


def position(geno_rows):
    block = lax.axis_index("snp")
    odd = lax.rem(block, 2)
    half = geno_rows // 2
    return block, odd, odd * half, (1 - odd) * half


def column_sum(values):
    return jnp.sum(values, axis=0, keepdims=True)


def copies_in(source, begin, target, sems, pieces):
    rows = target.shape[0] // pieces
    return [
        pltpu.make_async_copy(
            source.at[pl.ds(pl.multiple_of(begin + i * rows, 8), rows)],
            target.at[pl.ds(i * rows, rows)],
            sems.at[i],
        )
        for i in range(pieces)
    ]


def start(*groups):
    for group in groups:
        for copy in group:
            copy.start()


def finish(*copies):
    for copy in copies:
        copy.wait()


def copy_kernel(geno, out, sems):
    sent_at = position(geno.shape[0])[2]
    copies = copies_in(geno, sent_at, out, sems, READS)
    start(copies)
    finish(*copies)


def stat_kernel(
    geno,
    starts,
    ends,
    sent,
    pack,
    means,
    products,
    values,
    edges,
    sems,
    edge_sems,
):
    del sent
    rows, width = values.shape
    piece = rows // READS
    copies = copies_in(geno, 0, values, sems, READS)
    edge_copies = [
        pltpu.make_async_copy(ref, edges.at[pl.ds(i, 1)], edge_sems.at[i])
        for i, ref in enumerate((starts, ends))
    ]
    start(copies, edge_copies)
    for i, copy in enumerate(copies):
        copy.wait()
        at = slice(i * piece, (i + 1) * piece)
        if i == 0:
            centre = column_sum(values[at]) / piece
        near_centre = values[at] - centre
        part, squares = column_sum(near_centre), column_sum(near_centre * near_centre)
        high, low = split(near_centre)
        product = dot(high, high * 0.5, 0, 0) + dot(high, low, 0, 0)
        if i == 0:
            total, spread = part, squares
            products[...] = product
        else:
            total, spread = total + part, spread + squares
            products[...] += product
    offset = total / rows
    mean = centre + offset
    spread = spread - rows * offset * offset
    means[...] = jnp.concatenate([mean, offset, jnp.zeros((6, width), F32)], axis=0)
    tiles = width // LANES
    here = edges.shape[1]
    slot = (
        lax.broadcasted_iota(jnp.int32, (tiles, LANES), 0) * (LANES // here)
        + lax.broadcasted_iota(jnp.int32, (tiles, LANES), 1) // here
    )
    mine = slot == lax.axis_index("samp")
    finish(*edge_copies)

    def spread_out(i):
        row = jnp.concatenate([edges[i : i + 1].astype(F32)] * (LANES // here), axis=1)
        return jnp.where(mine, jnp.broadcast_to(row, (tiles, LANES)), jnp.float32(0.0))

    rows_out = [
        vector[:, t * LANES : (t + 1) * LANES] for vector in (mean, spread) for t in range(tiles)
    ]
    rows_out += [spread_out(0), spread_out(1)]
    pack[...] = jnp.broadcast_to(jnp.concatenate(rows_out, axis=0)[None], pack.shape)


def combine_kernel(packs, effect, sent_last, later, own, *, samples_here):
    count, _, _ = packs.shape
    columns, width = effect.shape
    tiles = width // LANES
    total = samples_here * count
    values = packs[...]
    means = values[:, :tiles]
    mean = jnp.sum(means, axis=0) / count
    spread = jnp.sum(values[:, tiles : 2 * tiles], axis=0)
    spread = spread + samples_here * jnp.sum((means - mean[None]) ** 2, axis=0)
    scale = lax.rsqrt(spread / total + EPSILON)
    starts = jnp.sum(values[:, 2 * tiles : 3 * tiles], axis=0)
    ends = jnp.sum(values[:, 3 * tiles :], axis=0)

    def as_row(tiled):
        return jnp.concatenate([tiled[t : t + 1] for t in range(tiles)], axis=1)

    scale_row = as_row(scale)
    info = jnp.concatenate(
        [as_row(mean), scale_row, as_row(starts), as_row(ends), jnp.zeros((4, width), F32)],
        axis=0,
    )
    scaled = effect[...] * scale_row
    own[:columns] = scaled
    own[columns:] = info
    rows = sent_last.shape[0]
    later[:rows] = sent_last[...]
    later[rows : rows + columns] = scaled
    later[rows + columns :] = info


def in_triangle(width, reaches_right, work):
    lower, upper, every = slice(0, width // 2), slice(width // 2, width), slice(0, width)

    @pl.when(reaches_right)
    def _():
        work([(lower, lower), (upper, every)], True)

    @pl.when(jnp.logical_not(reaches_right))
    def _():
        work([(lower, every), (upper, upper)], False)


def block_dots(left, right, rows, cols):
    return three_dots([part[:, rows] for part in left], [part[:, cols] for part in right], 0, 0)


def mate_kernel(
    geno,
    mate,
    means,
    half_products,
    products,
    mate_means,
    own_out,
    sent_last,
    values,
    mate_values,
    own_products,
    sems,
    mate_sems,
    out_sem,
):
    rows, width = values.shape
    _, odd, sent_at, _ = position(rows)
    last_at = pl.multiple_of(sent_at + rows // 2 - LAST_ROWS, 8)
    copies = copies_in(geno, 0, values, sems, READS)
    mate_copies = copies_in(mate, 0, mate_values, mate_sems, READS)
    for copy, mate_copy in zip(copies, mate_copies):
        copy.start()
        mate_copy.start()
    mean, offset = means[0:1], means[1:2]
    own_products[...] = (
        half_products[...]
        + half_products[...].T
        - (rows * jnp.broadcast_to(offset, (8, width)).T[:, 0:1]) * offset
    )
    write = pltpu.make_async_copy(own_products, own_out, out_sem.at[0])
    write.start()
    piece = rows // READS
    centre = None
    total = None
    for i in range(READS):
        at = slice(i * piece, (i + 1) * piece)
        copies[i].wait()
        mate_copies[i].wait()
        part = column_sum(mate_values[at])
        total = part if total is None else total + part
        centre = part / piece if centre is None else centre

        def work(blocks, right_side):
            left, right = split(values[at] - mean), split(mate_values[at] - centre)
            for block_rows, block_cols in blocks:
                product = block_dots(left, right, block_rows, block_cols)
                if i == 0:
                    products[block_rows, block_cols] = product
                else:
                    products[block_rows, block_cols] += product

        in_triangle(width, odd == 0, work)
    mate_means[...] = jnp.broadcast_to(total / rows, mate_means.shape)
    sent_last[...] = values[pl.ds(last_at, LAST_ROWS), :]
    write.wait()


def index_of(first, shape, dim):
    return (first + lax.broadcasted_iota(jnp.int32, shape, dim)).astype(F32)


def band_dot(keep, centred, source, cols, columns):
    band = jnp.where(keep, centred, jnp.float32(0.0))
    return three_dots(split(band), split(source[:columns, cols]), 1, 1)


def near_kernel(
    geno, means, mate_products, mate_means, own, mate, out, kept, kept_sems, *, columns, samples_here
):
    width = mate_products.shape[0]
    block, odd, _, kept_at = position(samples_here)
    kept_copies = copies_in(geno, kept_at, kept, kept_sems, 2)
    start(kept_copies)
    info = own[columns : columns + 4]
    shift = means[0:1] - info[0:1]
    by_row = jnp.concatenate([info, shift, jnp.zeros((3, width), F32)], axis=0).T
    row_shift = samples_here * by_row[:, 4:5]
    starts, ends = by_row[:, 2:3], by_row[:, 3:4]
    mate_shift = mate_means[0:1] - mate[columns : columns + 1]
    mate_block = block + 1 - 2 * odd

    def mate_work(blocks, right_side):
        for at, cols in blocks:
            centred = mate_products[at, cols] + row_shift[at] * mate_shift[:, cols]
            index = index_of(mate_block * width + cols.start, (1, centred.shape[1]), 1)
            keep = index < ends[at] if right_side else index >= starts[at]
            out[at] = band_dot(keep, centred, mate, cols, columns)

    in_triangle(width, odd == 0, mate_work)
    finish(*kept_copies)


def cross_kernel(
    kept,
    means,
    across,
    own_products,
    own,
    near,
    products,
    cross_means,
    near_sum,
    others,
    sems,
    *,
    columns,
    samples_here,
):
    rows, width = others.shape
    block, odd = position(rows)[:2]
    pieces = sems.shape[0]
    piece = rows // pieces
    copies = copies_in(across, 0, others, sems, pieces)
    start(copies)
    mean = means[0:1]
    info = own[columns : columns + 4]
    shift = mean - info[0:1]
    by_row = jnp.concatenate([info, shift, jnp.zeros((3, width), F32)], axis=0).T
    centred = own_products[...] + (samples_here * by_row[:, 4:5]) * shift
    index = index_of(block * width, (1, width), 1)
    keep = (index >= by_row[:, 2:3]) & (index < by_row[:, 3:4])
    near_sum[...] = near[...] + band_dot(keep, centred, own, slice(0, width), columns)
    centre = None
    for i, copy in enumerate(copies):
        copy.wait()
        at = slice(i * piece, (i + 1) * piece)
        part = column_sum(others[at])
        other_sum = part if i == 0 else other_sum + part
        centre = part / piece if i == 0 else centre

        def work(blocks, right_side):
            left = kept[at] - mean
            total = column_sum(left)
            if i == 0:
                cross_means[0:1] = total
            else:
                cross_means[0:1] += total
            left, right = split(left), split(others[at] - centre)
            for block_rows, block_cols in blocks:
                product = block_dots(left, right, block_rows, block_cols)
                if i == 0:
                    products[block_rows, block_cols] = product
                else:
                    products[block_rows, block_cols] += product

        in_triangle(width, odd == 1, work)
    cross_means[1:2] = other_sum / rows
    cross_means[2:3] = centre
    cross_means[3:] = jnp.zeros((5, width), F32)


def far_kernel(
    kept,
    products,
    means,
    cross_means,
    later,
    own,
    near,
    out,
    own_sum,
    far_sum,
    *,
    columns,
    total,
):
    half, width = kept.shape
    rows = later.shape[0] - own.shape[0]
    first_rows = half - rows
    block, odd = position(half)[:2]
    mean = own[columns : columns + 1]
    info = later[rows + columns : rows + columns + 4]
    far_mean, far_scale = info[0:1], info[1:2]
    shift = means[0:1] - mean
    by_row = jnp.concatenate(
        [own[columns : columns + 4], cross_means[0:1], shift, jnp.zeros((2, width), F32)], axis=0
    ).T
    row_scale = by_row[:, 1:2] * (1.0 / total)
    left_sum, row_shift = by_row[:, 4:5], first_rows * by_row[:, 5:6]
    centre_shift = cross_means[2:3] - far_mean
    other_shift = cross_means[1:2] - far_mean
    far_block = block + 2 * odd - 1
    count, _, piece_rows, lanes = out.shape

    def pieces_of(values):
        parts = values.reshape(count, 2, piece_rows, columns)
        return jnp.concatenate([parts[:, 0], parts[:, 1]], axis=-1)

    far_sum[...] = jnp.zeros_like(far_sum)

    def work(blocks, right_side):
        left, right = split(kept[first_rows:] - mean), split(later[:rows] - far_mean)
        for at, cols in blocks:
            centred = products[at, cols] + block_dots(left, right, at, cols)
            centred = centred + left_sum[at] * centre_shift[:, cols]
            centred = centred + row_shift[at] * other_shift[:, cols]
            row_index = index_of(block * width + at.start, (centred.shape[0], 1), 0)
            col_index = index_of(far_block * width + cols.start, (1, centred.shape[1]), 1)
            if right_side:
                keep_own = col_index < by_row[at, 3:4]
                keep_far = row_index >= info[2:3, cols]
            else:
                keep_own = col_index >= by_row[at, 2:3]
                keep_far = row_index < info[3:4, cols]
            own_sum[at] = near[at] + band_dot(
                keep_own, centred, later[rows : rows + columns], cols, columns
            )
            far_band = jnp.where(keep_far, centred, jnp.float32(0.0))
            far_sum[:, cols] += three_dots(split(own[:columns, at]), split(far_band), 1, 0)

    in_triangle(width, odd == 1, work)
    out[:, 1 - odd] = pieces_of(own_sum[...] * row_scale)
    out[:, odd] = pieces_of((far_sum[...] * (far_scale * (1.0 / total))).T)


def last_kernel(parts, out):
    total = jnp.sum(parts[...], axis=0)
    rows, columns = out.shape
    out[: rows // 2] = total[:, :columns]
    out[rows // 2 :] = total[:, columns:]


def call(kernel, shapes, specs, scratch=(), flops=1000, out_specs=None, aliases=None, **sizes):
    outs = [shape if hasattr(shape, "dtype") else jax.ShapeDtypeStruct(shape, F32) for shape in shapes]
    return pl.pallas_call(
        functools.partial(kernel, **sizes),
        out_shape=outs,
        in_specs=specs,
        out_specs=out_specs or [VMEM] * len(outs),
        scratch_shapes=list(scratch),
        input_output_aliases=aliases or {},
        compiler_params=pltpu.CompilerParams(vmem_limit_bytes=48 * 1024 * 1024),
        cost_estimate=pl.CostEstimate(flops=flops, bytes_accessed=1000, transcendentals=0),
        name=kernel.__name__,
    )


def body(genotype, effect, window_start, window_end):
    samp_count = lax.axis_size("samp")
    snp_count = lax.axis_size("snp")
    samples_here, width = genotype.shape
    columns = effect.shape[1]
    row_count = width // samp_count
    total = samples_here * samp_count
    half = samples_here // 2
    info_rows = columns + 8
    gram_flops = 6 * width * width * samples_here
    chip_pairs = [(i, i ^ 1) for i in range(snp_count)]
    cross = [(i, (i + 1) % snp_count) for i in range(1, snp_count, 2)]
    cross_pairs = [pair for i, j in cross[:-1] for pair in ((i, j), (j, i))]
    effect_rows = effect.T
    square = (width, width)
    whole = (samples_here, width)
    in_hbm = pltpu.with_memory_space_constraint(genotype, pltpu.HBM)
    reads = pltpu.SemaphoreType.DMA((READS,))

    sent = call(copy_kernel, [(half - LAST_ROWS, width)], [HBM], [reads])(in_hbm)[0]
    across = lax.ppermute(sent, "snp", cross_pairs)
    mate = lax.ppermute(genotype, "snp", chip_pairs)
    pack, means, half_products = call(
        stat_kernel,
        [
            (samp_count, 4 * width // LANES, LANES),
            (8, width),
            square,
        ],
        [HBM, HBM, HBM, ANY],
        [
            pltpu.VMEM(whole, F32),
            pltpu.VMEM((2, row_count), jnp.int32),
            reads,
            pltpu.SemaphoreType.DMA((2,)),
        ],
    )(
        in_hbm,
        pltpu.with_memory_space_constraint(window_start[None], pltpu.HBM),
        pltpu.with_memory_space_constraint(window_end[None], pltpu.HBM),
        sent,
    )
    packs = lax.all_to_all(pack, "samp", 0, 0)
    mate_products, mate_means, own_products, sent_last = call(
        mate_kernel,
        [square, (8, width), pltpu.HBM(square, F32), (LAST_ROWS, width)],
        [HBM, HBM, VMEM, VMEM],
        [
            pltpu.VMEM(whole, F32),
            pltpu.VMEM(whole, F32),
            pltpu.VMEM(square, F32),
            reads,
            reads,
            pltpu.SemaphoreType.DMA((1,)),
        ],
        out_specs=[VMEM, VMEM, HBM, VMEM],
        flops=2 * gram_flops,
        aliases={3: 0},
    )(in_hbm, pltpu.with_memory_space_constraint(mate, pltpu.HBM), means, half_products)
    later, own = call(
        combine_kernel,
        [(LAST_ROWS + info_rows, width), (info_rows, width)],
        [VMEM] * 3,
        samples_here=samples_here,
    )(packs, effect_rows, sent_last)
    far = lax.ppermute(later, "snp", cross_pairs)
    mate_info = lax.ppermute(own, "snp", chip_pairs)
    near, kept = call(
        near_kernel,
        [(width, columns), (half, width)],
        [HBM] + [VMEM] * 5,
        [pltpu.SemaphoreType.DMA((2,))],
        columns=columns,
        samples_here=samples_here,
    )(in_hbm, means, mate_products, mate_means, own, mate_info)
    cross_products, cross_means, near = call(
        cross_kernel,
        [square, (8, width), (width, columns)],
        [VMEM, VMEM, HBM] + [VMEM] * 3,
        [pltpu.VMEM((half - LAST_ROWS, width), F32), pltpu.SemaphoreType.DMA((FAR_READS,))],
        columns=columns,
        samples_here=samples_here,
        flops=gram_flops,
    )(kept, means, pltpu.with_memory_space_constraint(across, pltpu.HBM), own_products, own, near)
    sums = call(
        far_kernel,
        [(samp_count, 2, row_count // 2, 2 * columns)],
        [VMEM] * 7,
        [pltpu.VMEM((width, columns), F32), pltpu.VMEM((columns, width), F32)],
        columns=columns,
        total=total,
    )(kept, cross_products, means, cross_means, far, own, near)[0]
    groups = [[s * snp_count + i for s in range(samp_count) for i in pair] for pair in cross]
    parts = lax.all_to_all(
        sums.reshape(2 * samp_count, row_count // 2, 2 * columns),
        ("samp", "snp"),
        0,
        0,
        axis_index_groups=groups,
    )
    return call(last_kernel, [(row_count, columns)], [VMEM])(parts)[0]


def solution(mesh):
    placed = (P("samp", "snp"), P("snp", None), P(("snp", "samp")), P(("snp", "samp")))
    return jax.shard_map(
        body, mesh=mesh, in_specs=placed, out_specs=P(("snp", "samp"), None), check_vma=False
    )
```

```python
import functools

import jax
import jax.numpy as jnp
from jax import lax
from jax.experimental import pallas as pl
from jax.experimental.pallas import tpu as pltpu
from jax.sharding import PartitionSpec as P

EPSILON = 1e-05
F32 = jnp.float32
BF16 = jnp.bfloat16
LANES = 128
READS = 4
FAR_READS = 2
LAST_ROWS = 64
VMEM = pl.BlockSpec(memory_space=pltpu.VMEM)
HBM = pl.BlockSpec(memory_space=pltpu.HBM)
ANY = pl.BlockSpec(memory_space=pl.ANY)


def split(values):
    high = values.astype(BF16)
    return high, (values - high.astype(F32)).astype(BF16)


def dot(left, right, left_dim, right_dim):
    return lax.dot_general(
        left, right, (((left_dim,), (right_dim,)), ((), ())), preferred_element_type=F32
    )


def three_dots(left, right, left_dim, right_dim):
    (left_high, left_low), (right_high, right_low) = left, right
    return (
        dot(left_high, right_high, left_dim, right_dim)
        + dot(left_high, right_low, left_dim, right_dim)
        + dot(left_low, right_high, left_dim, right_dim)
    )


def position(geno_rows):
    block = lax.axis_index("snp")
    odd = lax.rem(block, 2)
    half = geno_rows // 2
    return block, odd, odd * half, (1 - odd) * half


def column_sum(values):
    return jnp.sum(values, axis=0, keepdims=True)


def copies_in(source, begin, target, sems, pieces):
    rows = target.shape[0] // pieces
    return [
        pltpu.make_async_copy(
            source.at[pl.ds(pl.multiple_of(begin + i * rows, 8), rows)],
            target.at[pl.ds(i * rows, rows)],
            sems.at[i],
        )
        for i in range(pieces)
    ]


def start(*groups):
    for group in groups:
        for copy in group:
            copy.start()


def finish(*copies):
    for copy in copies:
        copy.wait()


def copy_kernel(geno, out, sems):
    sent_at = position(geno.shape[0])[2]
    copies = copies_in(geno, sent_at, out, sems, READS)
    start(copies)
    finish(*copies)


def stat_kernel(
    geno,
    starts,
    ends,
    sent,
    pack,
    means,
    products,
    values,
    edges,
    sems,
    edge_sems,
):
    del sent
    rows, width = values.shape
    piece = rows // READS
    copies = copies_in(geno, 0, values, sems, READS)
    edge_copies = [
        pltpu.make_async_copy(ref, edges.at[pl.ds(i, 1)], edge_sems.at[i])
        for i, ref in enumerate((starts, ends))
    ]
    start(copies, edge_copies)
    for i, copy in enumerate(copies):
        copy.wait()
        at = slice(i * piece, (i + 1) * piece)
        if i == 0:
            centre = column_sum(values[at]) / piece
        near_centre = values[at] - centre
        part, squares = column_sum(near_centre), column_sum(near_centre * near_centre)
        high, low = split(near_centre)
        product = dot(high, high * 0.5, 0, 0) + dot(high, low, 0, 0)
        if i == 0:
            total, spread = part, squares
            products[...] = product
        else:
            total, spread = total + part, spread + squares
            products[...] += product
    offset = total / rows
    mean = centre + offset
    spread = spread - rows * offset * offset
    means[...] = jnp.concatenate([mean, offset, jnp.zeros((6, width), F32)], axis=0)
    tiles = width // LANES
    here = edges.shape[1]
    slot = (
        lax.broadcasted_iota(jnp.int32, (tiles, LANES), 0) * (LANES // here)
        + lax.broadcasted_iota(jnp.int32, (tiles, LANES), 1) // here
    )
    mine = slot == lax.axis_index("samp")
    finish(*edge_copies)

    def spread_out(i):
        row = jnp.concatenate([edges[i : i + 1].astype(F32)] * (LANES // here), axis=1)
        return jnp.where(mine, jnp.broadcast_to(row, (tiles, LANES)), jnp.float32(0.0))

    rows_out = [
        vector[:, t * LANES : (t + 1) * LANES] for vector in (mean, spread) for t in range(tiles)
    ]
    rows_out += [spread_out(0), spread_out(1)]
    pack[...] = jnp.broadcast_to(jnp.concatenate(rows_out, axis=0)[None], pack.shape)


def combine_kernel(packs, effect, sent_last, later, own, *, samples_here):
    count, _, _ = packs.shape
    columns, width = effect.shape
    tiles = width // LANES
    total = samples_here * count
    values = packs[...]
    means = values[:, :tiles]
    mean = jnp.sum(means, axis=0) / count
    spread = jnp.sum(values[:, tiles : 2 * tiles], axis=0)
    spread = spread + samples_here * jnp.sum((means - mean[None]) ** 2, axis=0)
    scale = lax.rsqrt(spread / total + EPSILON)
    starts = jnp.sum(values[:, 2 * tiles : 3 * tiles], axis=0)
    ends = jnp.sum(values[:, 3 * tiles :], axis=0)

    def as_row(tiled):
        return jnp.concatenate([tiled[t : t + 1] for t in range(tiles)], axis=1)

    scale_row = as_row(scale)
    info = jnp.concatenate(
        [as_row(mean), scale_row, as_row(starts), as_row(ends), jnp.zeros((4, width), F32)],
        axis=0,
    )
    scaled = effect[...] * scale_row
    own[:columns] = scaled
    own[columns:] = info
    rows = sent_last.shape[0]
    later[:rows] = sent_last[...]
    later[rows : rows + columns] = scaled
    later[rows + columns :] = info


def in_triangle(width, reaches_right, work):
    lower, upper, every = slice(0, width // 2), slice(width // 2, width), slice(0, width)

    @pl.when(reaches_right)
    def _():
        work([(lower, lower), (upper, every)], True)

    @pl.when(jnp.logical_not(reaches_right))
    def _():
        work([(lower, every), (upper, upper)], False)


def block_dots(left, right, rows, cols):
    return three_dots([part[:, rows] for part in left], [part[:, cols] for part in right], 0, 0)


def mate_kernel(
    geno,
    mate,
    means,
    half_products,
    products,
    mate_means,
    own_out,
    sent_last,
    values,
    mate_values,
    own_products,
    sems,
    mate_sems,
    out_sem,
):
    rows, width = values.shape
    _, odd, sent_at, _ = position(rows)
    last_at = pl.multiple_of(sent_at + rows // 2 - LAST_ROWS, 8)
    copies = copies_in(geno, 0, values, sems, READS)
    mate_copies = copies_in(mate, 0, mate_values, mate_sems, READS)
    for copy, mate_copy in zip(copies, mate_copies):
        copy.start()
        mate_copy.start()
    mean, offset = means[0:1], means[1:2]
    own_products[...] = (
        half_products[...]
        + half_products[...].T
        - (rows * jnp.broadcast_to(offset, (8, width)).T[:, 0:1]) * offset
    )
    write = pltpu.make_async_copy(own_products, own_out, out_sem.at[0])
    write.start()
    piece = rows // READS
    centre = None
    total = None
    for i in range(READS):
        at = slice(i * piece, (i + 1) * piece)
        copies[i].wait()
        mate_copies[i].wait()
        part = column_sum(mate_values[at])
        total = part if total is None else total + part
        centre = part / piece if centre is None else centre

        def work(blocks, right_side):
            left, right = split(values[at] - mean), split(mate_values[at] - centre)
            for block_rows, block_cols in blocks:
                product = block_dots(left, right, block_rows, block_cols)
                if i == 0:
                    products[block_rows, block_cols] = product
                else:
                    products[block_rows, block_cols] += product

        in_triangle(width, odd == 0, work)
    mate_means[...] = jnp.broadcast_to(total / rows, mate_means.shape)
    sent_last[...] = values[pl.ds(last_at, LAST_ROWS), :]
    write.wait()


def index_of(first, shape, dim):
    return (first + lax.broadcasted_iota(jnp.int32, shape, dim)).astype(F32)


def band_dot(keep, centred, source, cols, columns):
    band = jnp.where(keep, centred, jnp.float32(0.0))
    return three_dots(split(band), split(source[:columns, cols]), 1, 1)


def near_kernel(
    geno, means, mate_products, mate_means, own, mate, out, kept, kept_sems, *, columns, samples_here
):
    width = mate_products.shape[0]
    block, odd, _, kept_at = position(samples_here)
    kept_copies = copies_in(geno, kept_at, kept, kept_sems, 2)
    start(kept_copies)
    info = own[columns : columns + 4]
    shift = means[0:1] - info[0:1]
    by_row = jnp.concatenate([info, shift, jnp.zeros((3, width), F32)], axis=0).T
    row_shift = samples_here * by_row[:, 4:5]
    starts, ends = by_row[:, 2:3], by_row[:, 3:4]
    mate_shift = mate_means[0:1] - mate[columns : columns + 1]
    mate_block = block + 1 - 2 * odd

    def mate_work(blocks, right_side):
        for at, cols in blocks:
            centred = mate_products[at, cols] + row_shift[at] * mate_shift[:, cols]
            index = index_of(mate_block * width + cols.start, (1, centred.shape[1]), 1)
            keep = index < ends[at] if right_side else index >= starts[at]
            out[at] = band_dot(keep, centred, mate, cols, columns)

    in_triangle(width, odd == 0, mate_work)
    finish(*kept_copies)


def cross_kernel(
    kept,
    means,
    across,
    own_products,
    own,
    near,
    products,
    cross_means,
    near_sum,
    others,
    sems,
    *,
    columns,
    samples_here,
):
    rows, width = others.shape
    block, odd = position(rows)[:2]
    pieces = sems.shape[0]
    piece = rows // pieces
    copies = copies_in(across, 0, others, sems, pieces)
    start(copies)
    mean = means[0:1]
    info = own[columns : columns + 4]
    shift = mean - info[0:1]
    by_row = jnp.concatenate([info, shift, jnp.zeros((3, width), F32)], axis=0).T
    centred = own_products[...] + (samples_here * by_row[:, 4:5]) * shift
    index = index_of(block * width, (1, width), 1)
    keep = (index >= by_row[:, 2:3]) & (index < by_row[:, 3:4])
    near_sum[...] = near[...] + band_dot(keep, centred, own, slice(0, width), columns)
    centre = None
    for i, copy in enumerate(copies):
        copy.wait()
        at = slice(i * piece, (i + 1) * piece)
        part = column_sum(others[at])
        other_sum = part if i == 0 else other_sum + part
        centre = part / piece if i == 0 else centre

        def work(blocks, right_side):
            left = kept[at] - mean
            total = column_sum(left)
            if i == 0:
                cross_means[0:1] = total
            else:
                cross_means[0:1] += total
            left, right = split(left), split(others[at] - centre)
            for block_rows, block_cols in blocks:
                product = block_dots(left, right, block_rows, block_cols)
                if i == 0:
                    products[block_rows, block_cols] = product
                else:
                    products[block_rows, block_cols] += product

        in_triangle(width, odd == 1, work)
    cross_means[1:2] = other_sum / rows
    cross_means[2:3] = centre
    cross_means[3:] = jnp.zeros((5, width), F32)


def far_kernel(
    kept,
    products,
    means,
    cross_means,
    later,
    own,
    near,
    out,
    own_sum,
    far_sum,
    *,
    columns,
    total,
):
    half, width = kept.shape
    rows = later.shape[0] - own.shape[0]
    first_rows = half - rows
    block, odd = position(half)[:2]
    mean = own[columns : columns + 1]
    info = later[rows + columns : rows + columns + 4]
    far_mean, far_scale = info[0:1], info[1:2]
    shift = means[0:1] - mean
    by_row = jnp.concatenate(
        [own[columns : columns + 4], cross_means[0:1], shift, jnp.zeros((2, width), F32)], axis=0
    ).T
    row_scale = by_row[:, 1:2] * (1.0 / total)
    left_sum, row_shift = by_row[:, 4:5], first_rows * by_row[:, 5:6]
    centre_shift = cross_means[2:3] - far_mean
    other_shift = cross_means[1:2] - far_mean
    far_block = block + 2 * odd - 1
    count, _, piece_rows, lanes = out.shape

    def pieces_of(values):
        parts = values.reshape(count, 2, piece_rows, columns)
        return jnp.concatenate([parts[:, 0], parts[:, 1]], axis=-1)

    at_end = (block == 0) | (block == lax.axis_size("snp") - 1)
    far_factor = jnp.where(at_end, 0.0, 1.0 / total)
    far_sum[...] = jnp.zeros_like(far_sum)

    def work(blocks, right_side):
        left, right = split(kept[first_rows:] - mean), split(later[:rows] - far_mean)
        for at, cols in blocks:
            centred = products[at, cols] + block_dots(left, right, at, cols)
            centred = centred + left_sum[at] * centre_shift[:, cols]
            centred = centred + row_shift[at] * other_shift[:, cols]
            row_index = index_of(block * width + at.start, (centred.shape[0], 1), 0)
            col_index = index_of(far_block * width + cols.start, (1, centred.shape[1]), 1)
            if right_side:
                keep_own = col_index < by_row[at, 3:4]
                keep_far = row_index >= info[2:3, cols]
            else:
                keep_own = col_index >= by_row[at, 2:3]
                keep_far = row_index < info[3:4, cols]
            own_sum[at] = near[at] + band_dot(
                keep_own, centred, later[rows : rows + columns], cols, columns
            )
            far_band = jnp.where(keep_far, centred, jnp.float32(0.0))
            far_sum[:, cols] += three_dots(split(own[:columns, at]), split(far_band), 1, 0)

    in_triangle(width, odd == 1, work)
    out[:, 1 - odd] = pieces_of(own_sum[...] * row_scale)
    out[:, odd] = pieces_of((far_sum[...] * (far_scale * far_factor)).T)


def last_kernel(parts, out):
    total = jnp.sum(parts[...], axis=0)
    rows, columns = out.shape
    out[: rows // 2] = total[:, :columns]
    out[rows // 2 :] = total[:, columns:]


def call(kernel, shapes, specs, scratch=(), flops=1000, out_specs=None, aliases=None, **sizes):
    outs = [shape if hasattr(shape, "dtype") else jax.ShapeDtypeStruct(shape, F32) for shape in shapes]
    return pl.pallas_call(
        functools.partial(kernel, **sizes),
        out_shape=outs,
        in_specs=specs,
        out_specs=out_specs or [VMEM] * len(outs),
        scratch_shapes=list(scratch),
        input_output_aliases=aliases or {},
        compiler_params=pltpu.CompilerParams(vmem_limit_bytes=48 * 1024 * 1024),
        cost_estimate=pl.CostEstimate(flops=flops, bytes_accessed=1000, transcendentals=0),
        name=kernel.__name__,
    )


def body(genotype, effect, window_start, window_end):
    samp_count = lax.axis_size("samp")
    snp_count = lax.axis_size("snp")
    samples_here, width = genotype.shape
    columns = effect.shape[1]
    row_count = width // samp_count
    total = samples_here * samp_count
    half = samples_here // 2
    info_rows = columns + 8
    gram_flops = 6 * width * width * samples_here
    chip_pairs = [(i, i ^ 1) for i in range(snp_count)]
    cross = [(i, (i + 1) % snp_count) for i in range(1, snp_count, 2)]
    cross_pairs = [pair for i, j in cross for pair in ((i, j), (j, i))]
    effect_rows = effect.T
    square = (width, width)
    whole = (samples_here, width)
    in_hbm = pltpu.with_memory_space_constraint(genotype, pltpu.HBM)
    reads = pltpu.SemaphoreType.DMA((READS,))

    sent = call(copy_kernel, [(half - LAST_ROWS, width)], [HBM], [reads])(in_hbm)[0]
    across = lax.ppermute(sent, "snp", cross_pairs)
    mate = lax.ppermute(genotype, "snp", chip_pairs)
    pack, means, half_products = call(
        stat_kernel,
        [
            (samp_count, 4 * width // LANES, LANES),
            (8, width),
            square,
        ],
        [HBM, HBM, HBM, ANY],
        [
            pltpu.VMEM(whole, F32),
            pltpu.VMEM((2, row_count), jnp.int32),
            reads,
            pltpu.SemaphoreType.DMA((2,)),
        ],
    )(
        in_hbm,
        pltpu.with_memory_space_constraint(window_start[None], pltpu.HBM),
        pltpu.with_memory_space_constraint(window_end[None], pltpu.HBM),
        sent,
    )
    packs = lax.all_to_all(pack, "samp", 0, 0)
    mate_products, mate_means, own_products, sent_last = call(
        mate_kernel,
        [square, (8, width), pltpu.HBM(square, F32), (LAST_ROWS, width)],
        [HBM, HBM, VMEM, VMEM],
        [
            pltpu.VMEM(whole, F32),
            pltpu.VMEM(whole, F32),
            pltpu.VMEM(square, F32),
            reads,
            reads,
            pltpu.SemaphoreType.DMA((1,)),
        ],
        out_specs=[VMEM, VMEM, HBM, VMEM],
        flops=2 * gram_flops,
        aliases={3: 0},
    )(in_hbm, pltpu.with_memory_space_constraint(mate, pltpu.HBM), means, half_products)
    later, own = call(
        combine_kernel,
        [(LAST_ROWS + info_rows, width), (info_rows, width)],
        [VMEM] * 3,
        samples_here=samples_here,
    )(packs, effect_rows, sent_last)
    far = lax.ppermute(later, "snp", cross_pairs)
    mate_info = lax.ppermute(own, "snp", chip_pairs)
    near, kept = call(
        near_kernel,
        [(width, columns), (half, width)],
        [HBM] + [VMEM] * 5,
        [pltpu.SemaphoreType.DMA((2,))],
        columns=columns,
        samples_here=samples_here,
    )(in_hbm, means, mate_products, mate_means, own, mate_info)
    cross_products, cross_means, near = call(
        cross_kernel,
        [square, (8, width), (width, columns)],
        [VMEM, VMEM, HBM] + [VMEM] * 3,
        [pltpu.VMEM((half - LAST_ROWS, width), F32), pltpu.SemaphoreType.DMA((FAR_READS,))],
        columns=columns,
        samples_here=samples_here,
        flops=gram_flops,
    )(kept, means, pltpu.with_memory_space_constraint(across, pltpu.HBM), own_products, own, near)
    sums = call(
        far_kernel,
        [(samp_count, 2, row_count // 2, 2 * columns)],
        [VMEM] * 7,
        [pltpu.VMEM((width, columns), F32), pltpu.VMEM((columns, width), F32)],
        columns=columns,
        total=total,
    )(kept, cross_products, means, cross_means, far, own, near)[0]
    groups = [[s * snp_count + i for s in range(samp_count) for i in pair] for pair in cross]
    parts = lax.all_to_all(
        sums.reshape(2 * samp_count, row_count // 2, 2 * columns),
        ("samp", "snp"),
        0,
        0,
        axis_index_groups=groups,
    )
    return call(last_kernel, [(row_count, columns)], [VMEM])(parts)[0]


def solution(mesh):
    placed = (P("samp", "snp"), P("snp", None), P(("snp", "samp")), P(("snp", "samp")))
    return jax.shard_map(
        body, mesh=mesh, in_specs=placed, out_specs=P(("snp", "samp"), None), check_vma=False
    )
```

```python
import functools

import jax
import jax.numpy as jnp
from jax import lax
from jax.experimental import pallas as pl
from jax.experimental.pallas import tpu as pltpu
from jax.sharding import PartitionSpec as P

EPSILON = 1e-05
F32 = jnp.float32
BF16 = jnp.bfloat16
LANES = 128
READS = 4
FAR_READS = 2
LAST_ROWS = 64
VMEM = pl.BlockSpec(memory_space=pltpu.VMEM)
HBM = pl.BlockSpec(memory_space=pltpu.HBM)
ANY = pl.BlockSpec(memory_space=pl.ANY)


def split(values):
    high = values.astype(BF16)
    return high, (values - high.astype(F32)).astype(BF16)


def dot(left, right, left_dim, right_dim):
    return lax.dot_general(
        left, right, (((left_dim,), (right_dim,)), ((), ())), preferred_element_type=F32
    )


def three_dots(left, right, left_dim, right_dim):
    (left_high, left_low), (right_high, right_low) = left, right
    return (
        dot(left_high, right_high, left_dim, right_dim)
        + dot(left_high, right_low, left_dim, right_dim)
        + dot(left_low, right_high, left_dim, right_dim)
    )


def position(geno_rows):
    block = lax.axis_index("snp")
    odd = lax.rem(block, 2)
    half = geno_rows // 2
    return block, odd, odd * half, (1 - odd) * half


def column_sum(values):
    return jnp.sum(values, axis=0, keepdims=True)


def copies_in(source, begin, target, sems, pieces):
    rows = target.shape[0] // pieces
    return [
        pltpu.make_async_copy(
            source.at[pl.ds(pl.multiple_of(begin + i * rows, 8), rows)],
            target.at[pl.ds(i * rows, rows)],
            sems.at[i],
        )
        for i in range(pieces)
    ]


def start(*groups):
    for group in groups:
        for copy in group:
            copy.start()


def finish(*copies):
    for copy in copies:
        copy.wait()


def copy_kernel(geno, out, sems):
    sent_at = position(geno.shape[0])[2]
    copies = copies_in(geno, sent_at, out, sems, READS)
    start(copies)
    finish(*copies)


def stat_kernel(
    geno,
    starts,
    ends,
    sent,
    pack,
    means,
    products,
    values,
    edges,
    sems,
    edge_sems,
):
    del sent
    rows, width = values.shape
    piece = rows // READS
    copies = copies_in(geno, 0, values, sems, READS)
    edge_copies = [
        pltpu.make_async_copy(ref, edges.at[pl.ds(i, 1)], edge_sems.at[i])
        for i, ref in enumerate((starts, ends))
    ]
    start(copies, edge_copies)
    for i, copy in enumerate(copies):
        copy.wait()
        at = slice(i * piece, (i + 1) * piece)
        if i == 0:
            centre = column_sum(values[at]) / piece
        near_centre = values[at] - centre
        part, squares = column_sum(near_centre), column_sum(near_centre * near_centre)
        high, low = split(near_centre)
        product = dot(high, high * 0.5, 0, 0) + dot(high, low, 0, 0)
        if i == 0:
            total, spread = part, squares
            products[...] = product
        else:
            total, spread = total + part, spread + squares
            products[...] += product
    offset = total / rows
    mean = centre + offset
    spread = spread - rows * offset * offset
    means[...] = jnp.concatenate([mean, offset, jnp.zeros((6, width), F32)], axis=0)
    tiles = width // LANES
    here = edges.shape[1]
    slot = (
        lax.broadcasted_iota(jnp.int32, (tiles, LANES), 0) * (LANES // here)
        + lax.broadcasted_iota(jnp.int32, (tiles, LANES), 1) // here
    )
    mine = slot == lax.axis_index("samp")
    finish(*edge_copies)

    def spread_out(i):
        row = jnp.concatenate([edges[i : i + 1].astype(F32)] * (LANES // here), axis=1)
        return jnp.where(mine, jnp.broadcast_to(row, (tiles, LANES)), jnp.float32(0.0))

    rows_out = [
        vector[:, t * LANES : (t + 1) * LANES] for vector in (mean, spread) for t in range(tiles)
    ]
    rows_out += [spread_out(0), spread_out(1)]
    pack[...] = jnp.broadcast_to(jnp.concatenate(rows_out, axis=0)[None], pack.shape)


def combine_kernel(packs, effect, sent_last, later, own, *, samples_here):
    count, _, _ = packs.shape
    columns, width = effect.shape
    tiles = width // LANES
    total = samples_here * count
    values = packs[...]
    means = values[:, :tiles]
    mean = jnp.sum(means, axis=0) / count
    spread = jnp.sum(values[:, tiles : 2 * tiles], axis=0)
    spread = spread + samples_here * jnp.sum((means - mean[None]) ** 2, axis=0)
    scale = lax.rsqrt(spread / total + EPSILON)
    starts = jnp.sum(values[:, 2 * tiles : 3 * tiles], axis=0)
    ends = jnp.sum(values[:, 3 * tiles :], axis=0)

    def as_row(tiled):
        return jnp.concatenate([tiled[t : t + 1] for t in range(tiles)], axis=1)

    scale_row = as_row(scale)
    info = jnp.concatenate(
        [as_row(mean), scale_row, as_row(starts), as_row(ends), jnp.zeros((4, width), F32)],
        axis=0,
    )
    scaled = effect[...] * scale_row
    own[:columns] = scaled
    own[columns:] = info
    rows = sent_last.shape[0]
    later[:rows] = sent_last[...]
    later[rows : rows + columns] = scaled
    later[rows + columns :] = info


def in_triangle(width, reaches_right, work):
    lower, upper, every = slice(0, width // 2), slice(width // 2, width), slice(0, width)

    @pl.when(reaches_right)
    def _():
        work([(lower, lower), (upper, every)], True)

    @pl.when(jnp.logical_not(reaches_right))
    def _():
        work([(lower, every), (upper, upper)], False)


def block_dots(left, right, rows, cols):
    return three_dots([part[:, rows] for part in left], [part[:, cols] for part in right], 0, 0)


def mate_kernel(
    geno,
    mate,
    means,
    half_products,
    products,
    mate_means,
    own_out,
    sent_last,
    values,
    mate_values,
    own_products,
    sems,
    mate_sems,
    out_sem,
):
    rows, width = values.shape
    _, odd, sent_at, _ = position(rows)
    last_at = pl.multiple_of(sent_at + rows // 2 - LAST_ROWS, 8)
    copies = copies_in(geno, 0, values, sems, READS)
    mate_copies = copies_in(mate, 0, mate_values, mate_sems, READS)
    for copy, mate_copy in zip(copies, mate_copies):
        copy.start()
        mate_copy.start()
    mean, offset = means[0:1], means[1:2]
    own_products[...] = (
        half_products[...]
        + half_products[...].T
        - (rows * jnp.broadcast_to(offset, (8, width)).T[:, 0:1]) * offset
    )
    write = pltpu.make_async_copy(own_products, own_out, out_sem.at[0])
    write.start()
    piece = rows // READS
    centre = None
    total = None
    for i in range(READS):
        at = slice(i * piece, (i + 1) * piece)
        copies[i].wait()
        mate_copies[i].wait()
        part = column_sum(mate_values[at])
        total = part if total is None else total + part
        centre = part / piece if centre is None else centre

        def work(blocks, right_side):
            left, right = split(values[at] - mean), split(mate_values[at] - centre)
            for block_rows, block_cols in blocks:
                product = block_dots(left, right, block_rows, block_cols)
                if i == 0:
                    products[block_rows, block_cols] = product
                else:
                    products[block_rows, block_cols] += product

        in_triangle(width, odd == 0, work)
    mate_means[...] = jnp.broadcast_to(total / rows, mate_means.shape)
    sent_last[...] = values[pl.ds(last_at, LAST_ROWS), :]
    write.wait()


def index_of(first, shape, dim):
    return (first + lax.broadcasted_iota(jnp.int32, shape, dim)).astype(F32)


def band_dot(keep, centred, source, cols, columns):
    band = jnp.where(keep, centred, jnp.float32(0.0))
    return three_dots(split(band), split(source[:columns, cols]), 1, 1)


def near_kernel(
    geno, means, mate_products, mate_means, own, mate, out, kept, kept_sems, *, columns, samples_here
):
    width = mate_products.shape[0]
    block, odd, _, kept_at = position(samples_here)
    kept_copies = copies_in(geno, kept_at, kept, kept_sems, 1)
    start(kept_copies)
    info = own[columns : columns + 4]
    shift = means[0:1] - info[0:1]
    by_row = jnp.concatenate([info, shift, jnp.zeros((3, width), F32)], axis=0).T
    row_shift = samples_here * by_row[:, 4:5]
    starts, ends = by_row[:, 2:3], by_row[:, 3:4]
    mate_shift = mate_means[0:1] - mate[columns : columns + 1]
    mate_block = block + 1 - 2 * odd

    def mate_work(blocks, right_side):
        for at, cols in blocks:
            centred = mate_products[at, cols] + row_shift[at] * mate_shift[:, cols]
            index = index_of(mate_block * width + cols.start, (1, centred.shape[1]), 1)
            keep = index < ends[at] if right_side else index >= starts[at]
            out[at] = band_dot(keep, centred, mate, cols, columns)

    in_triangle(width, odd == 0, mate_work)
    finish(*kept_copies)


def cross_kernel(
    geno,
    kept_first,
    means,
    across,
    own_products,
    own,
    near,
    products,
    cross_means,
    near_sum,
    kept_last,
    others,
    sems,
    kept_sems,
    *,
    columns,
    samples_here,
):
    rows, width = others.shape
    block, odd, _, kept_at = position(geno.shape[0])
    pieces = sems.shape[0]
    piece = rows // pieces
    copies = copies_in(across, 0, others, sems, pieces)
    kept_copies = copies_in(geno, kept_at + piece, kept_last, kept_sems, 1)
    start(copies, kept_copies)
    mean = means[0:1]
    info = own[columns : columns + 4]
    shift = mean - info[0:1]
    by_row = jnp.concatenate([info, shift, jnp.zeros((3, width), F32)], axis=0).T
    centred = own_products[...] + (samples_here * by_row[:, 4:5]) * shift
    index = index_of(block * width, (1, width), 1)
    keep = (index >= by_row[:, 2:3]) & (index < by_row[:, 3:4])
    near_sum[...] = near[...] + band_dot(keep, centred, own, slice(0, width), columns)
    centre = None
    for i, copy in enumerate(copies):
        copy.wait()
        if i == 1:
            finish(*kept_copies)
        at = slice(i * piece, (i + 1) * piece)
        part = column_sum(others[at])
        other_sum = part if i == 0 else other_sum + part
        centre = part / piece if i == 0 else centre

        def work(blocks, right_side):
            left = (kept_last[:piece] if i else kept_first[...]) - mean
            total = column_sum(left)
            if i == 0:
                cross_means[0:1] = total
            else:
                cross_means[0:1] += total
            left, right = split(left), split(others[at] - centre)
            for block_rows, block_cols in blocks:
                product = block_dots(left, right, block_rows, block_cols)
                if i == 0:
                    products[block_rows, block_cols] = product
                else:
                    products[block_rows, block_cols] += product

        in_triangle(width, odd == 1, work)
    cross_means[1:2] = other_sum / rows
    cross_means[2:3] = centre
    cross_means[3:] = jnp.zeros((5, width), F32)


def far_kernel(
    kept,
    products,
    means,
    cross_means,
    later,
    own,
    near,
    out,
    own_sum,
    far_sum,
    *,
    columns,
    total,
    samples_here,
):
    half, width = samples_here // 2, own.shape[1]
    rows = later.shape[0] - own.shape[0]
    first_rows = half - rows
    block, odd = position(samples_here)[:2]
    mean = own[columns : columns + 1]
    info = later[rows + columns : rows + columns + 4]
    far_mean, far_scale = info[0:1], info[1:2]
    shift = means[0:1] - mean
    by_row = jnp.concatenate(
        [own[columns : columns + 4], cross_means[0:1], shift, jnp.zeros((2, width), F32)], axis=0
    ).T
    row_scale = by_row[:, 1:2] * (1.0 / total)
    left_sum, row_shift = by_row[:, 4:5], first_rows * by_row[:, 5:6]
    centre_shift = cross_means[2:3] - far_mean
    other_shift = cross_means[1:2] - far_mean
    far_block = block + 2 * odd - 1
    _, count, piece_rows, lanes = out.shape

    def pieces_of(values):
        parts = values.reshape(count, 2, piece_rows, columns)
        return jnp.concatenate([parts[:, 0], parts[:, 1]], axis=-1)

    at_end = (block == 0) | (block == lax.axis_size("snp") - 1)
    far_factor = jnp.where(at_end, 0.0, 1.0 / total)
    far_sum[...] = jnp.zeros_like(far_sum)

    def work(blocks, right_side):
        left, right = split(kept[kept.shape[0] - rows :] - mean), split(later[:rows] - far_mean)
        for at, cols in blocks:
            centred = products[at, cols] + block_dots(left, right, at, cols)
            centred = centred + left_sum[at] * centre_shift[:, cols]
            centred = centred + row_shift[at] * other_shift[:, cols]
            row_index = index_of(block * width + at.start, (centred.shape[0], 1), 0)
            col_index = index_of(far_block * width + cols.start, (1, centred.shape[1]), 1)
            if right_side:
                keep_own = col_index < by_row[at, 3:4]
                keep_far = row_index >= info[2:3, cols]
            else:
                keep_own = col_index >= by_row[at, 2:3]
                keep_far = row_index < info[3:4, cols]
            own_sum[at] = near[at] + band_dot(
                keep_own, centred, later[rows : rows + columns], cols, columns
            )
            far_band = jnp.where(keep_far, centred, jnp.float32(0.0))
            far_sum[:, cols] += three_dots(split(own[:columns, at]), split(far_band), 1, 0)

    in_triangle(width, odd == 1, work)
    out[1 - odd] = pieces_of(own_sum[...] * row_scale)
    out[odd] = pieces_of((far_sum[...] * (far_scale * far_factor)).T)


def last_kernel(parts, out):
    total = jnp.sum(parts[...], axis=0)
    rows, columns = out.shape
    out[: rows // 2] = total[:, :columns]
    out[rows // 2 :] = total[:, columns:]


def call(kernel, shapes, specs, scratch=(), flops=1000, out_specs=None, aliases=None, **sizes):
    outs = [shape if hasattr(shape, "dtype") else jax.ShapeDtypeStruct(shape, F32) for shape in shapes]
    return pl.pallas_call(
        functools.partial(kernel, **sizes),
        out_shape=outs,
        in_specs=specs,
        out_specs=out_specs or [VMEM] * len(outs),
        scratch_shapes=list(scratch),
        input_output_aliases=aliases or {},
        compiler_params=pltpu.CompilerParams(vmem_limit_bytes=48 * 1024 * 1024),
        cost_estimate=pl.CostEstimate(flops=flops, bytes_accessed=1000, transcendentals=0),
        name=kernel.__name__,
    )


def body(genotype, effect, window_start, window_end):
    samp_count = lax.axis_size("samp")
    snp_count = lax.axis_size("snp")
    samples_here, width = genotype.shape
    columns = effect.shape[1]
    row_count = width // samp_count
    total = samples_here * samp_count
    half = samples_here // 2
    info_rows = columns + 8
    gram_flops = 6 * width * width * samples_here
    chip_pairs = [(i, i ^ 1) for i in range(snp_count)]
    cross = [(i, (i + 1) % snp_count) for i in range(1, snp_count, 2)]
    cross_pairs = [pair for i, j in cross for pair in ((i, j), (j, i))]
    effect_rows = effect.T
    square = (width, width)
    whole = (samples_here, width)
    in_hbm = pltpu.with_memory_space_constraint(genotype, pltpu.HBM)
    reads = pltpu.SemaphoreType.DMA((READS,))

    sent = call(copy_kernel, [(half - LAST_ROWS, width)], [HBM], [reads])(in_hbm)[0]
    across = lax.ppermute(sent, "snp", cross_pairs)
    mate = lax.ppermute(genotype, "snp", chip_pairs)
    pack, means, half_products = call(
        stat_kernel,
        [
            (samp_count, 4 * width // LANES, LANES),
            (8, width),
            square,
        ],
        [HBM, HBM, HBM, ANY],
        [
            pltpu.VMEM(whole, F32),
            pltpu.VMEM((2, row_count), jnp.int32),
            reads,
            pltpu.SemaphoreType.DMA((2,)),
        ],
    )(
        in_hbm,
        pltpu.with_memory_space_constraint(window_start[None], pltpu.HBM),
        pltpu.with_memory_space_constraint(window_end[None], pltpu.HBM),
        sent,
    )
    packs = lax.all_to_all(pack, "samp", 0, 0)
    mate_products, mate_means, own_products, sent_last = call(
        mate_kernel,
        [square, (8, width), pltpu.HBM(square, F32), (LAST_ROWS, width)],
        [HBM, HBM, VMEM, VMEM],
        [
            pltpu.VMEM(whole, F32),
            pltpu.VMEM(whole, F32),
            pltpu.VMEM(square, F32),
            reads,
            reads,
            pltpu.SemaphoreType.DMA((1,)),
        ],
        out_specs=[VMEM, VMEM, HBM, VMEM],
        flops=2 * gram_flops,
        aliases={3: 0},
    )(in_hbm, pltpu.with_memory_space_constraint(mate, pltpu.HBM), means, half_products)
    later, own = call(
        combine_kernel,
        [(LAST_ROWS + info_rows, width), (info_rows, width)],
        [VMEM] * 3,
        samples_here=samples_here,
    )(packs, effect_rows, sent_last)
    far = lax.ppermute(later, "snp", cross_pairs)
    mate_info = lax.ppermute(own, "snp", chip_pairs)
    piece_rows = (half - LAST_ROWS) // FAR_READS
    near, kept = call(
        near_kernel,
        [(width, columns), (piece_rows, width)],
        [HBM] + [VMEM] * 5,
        [pltpu.SemaphoreType.DMA((1,))],
        columns=columns,
        samples_here=samples_here,
    )(in_hbm, means, mate_products, mate_means, own, mate_info)
    cross_products, cross_means, near, kept = call(
        cross_kernel,
        [square, (8, width), (width, columns), (half - piece_rows, width)],
        [HBM, VMEM, VMEM, HBM] + [VMEM] * 3,
        [
            pltpu.VMEM((half - LAST_ROWS, width), F32),
            pltpu.SemaphoreType.DMA((FAR_READS,)),
            pltpu.SemaphoreType.DMA((1,)),
        ],
        columns=columns,
        samples_here=samples_here,
        flops=gram_flops,
    )(in_hbm, kept, means, pltpu.with_memory_space_constraint(across, pltpu.HBM), own_products, own, near)
    sums = call(
        far_kernel,
        [(2, samp_count, row_count // 2, 2 * columns)],
        [VMEM] * 7,
        [pltpu.VMEM((width, columns), F32), pltpu.VMEM((columns, width), F32)],
        columns=columns,
        total=total,
        samples_here=samples_here,
    )(kept, cross_products, means, cross_means, far, own, near)[0]
    groups = [[s * snp_count + i for i in pair for s in range(samp_count)] for pair in cross]
    parts = lax.all_to_all(
        sums.reshape(2 * samp_count, row_count // 2, 2 * columns),
        ("samp", "snp"),
        0,
        0,
        axis_index_groups=groups,
    )
    return call(last_kernel, [(row_count, columns)], [VMEM])(parts)[0]


def solution(mesh):
    placed = (P("samp", "snp"), P("snp", None), P(("snp", "samp")), P(("snp", "samp")))
    return jax.shard_map(
        body, mesh=mesh, in_specs=placed, out_specs=P(("snp", "samp"), None), check_vma=False
    )
```
